32 devices in a mesh: section: 4 (over y, x), dom: 8 (over z, core).
Axes of the slice: x: 2, y: 2, z: 4, core: 2. Of those that a mesh axis runs over, the one named last changes fastest.
Arguments:
- measures: bfloat16 [131072, 128], P(('section', 'dom')), may hold values from -6 to 6
- pred_columns: int32 [2, 131072], P(None, ('section', 'dom')), may hold values from 0 to 99
- bounds: int32 [2, 2], replicated, may hold values from 0 to 100
- lengths: int32 [1024], P(('section', 'dom')), may hold values from 120 to 128
- destination: int32 [131072, 1], P(('section', 'dom')), may hold values from 0 to 31; in each aligned block of 4096 rows (0 to 4095, 4096 to 8191, ...) at most 256 rows name the same one
- key_offset: int32 [131072], P(('section', 'dom')), may hold values from 0 to 2047
- group_ids: int32 [131072], P(('section', 'dom')), may hold values from 0 to 1023
- build_table: bfloat16 [65536, 128], P(('section', 'dom')), may hold values from -6 to 6
Outputs:
- group_sums: float32 [1024, 128], P(('section', 'dom'))
- top_scores: float32 [16], replicated
The draws below stay inside these ranges and needn't reach their ends.
Inputs may be any that keep to these rules, and one draw needn't show every extreme that they name: Among the rows of one device, no destination is named more than 256 times, a bound that some block reaches.
All inputs are finite; a program needn't handle non-finite values.
Results may differ from the reference program's by a relative error of at most 0.0048.
Values may be sent and summed in bfloat16 or wider, within the bound.
A program may use at most 64 MiB of HBM per device.

```python
import math
import jax
import jax.numpy as jnp
import numpy as np
from jax import lax

F = 128
BLOCK = 128
NPRED = 2
TOPK = 16
ROWS_DEV = 4096
BUILD_DEV = 2048
TOTAL_ROWS = 131072
KEYS = 65536
GROUPS = 1024
CAP = 256
DEVICES = 32


def draw_bounds(key, part):
    lower_key = jax.random.fold_in(key, 11)
    upper_key = jax.random.fold_in(key, 23)
    lower = jax.random.randint(lower_key, (NPRED,), 0, 3, dtype=jnp.int32)
    upper = jax.random.randint(upper_key, (NPRED,), 98, 101, dtype=jnp.int32)
    return jnp.stack([lower, upper], axis=1)


def with_ends(array, rng, low, top_value):
    index_at = [jax.random.randint(jax.random.fold_in(rng, axis), (), 0, length) for axis, length in enumerate(array.shape)]
    longest = array.shape.index(max(array.shape))
    beside = index_at[:longest] + [(index_at[longest] + 1) % array.shape[longest]] + index_at[longest + 1:]
    return array.at[tuple(index_at)].set(low).at[tuple(beside)].set(top_value)


def block_scale(rng, shape, pieces, smallest, high):
    factor_of, own = 1.0, jax.random.fold_in(rng, 6)
    for dim, parts in pieces:
        steps = jnp.exp(jax.random.uniform(jax.random.fold_in(own, dim), (parts,), jnp.float32, smallest / len(pieces), high / len(pieces)))
        factor_of = factor_of * jnp.repeat(steps, shape[dim] // parts).reshape([-1 if axis == dim else 1 for axis in range(len(shape))])
    return factor_of


def assign_block(key, own, number, rows, number_of, top, bound, lean):
    order = jax.random.permutation(key, number_of)
    heavy_load, ordinary = load_shares(number_of, rows * top, bound, lean, True), load_shares(number_of, rows * top, bound, lean, False)
    places = jnp.arange(number_of)

    def named(sizes, offset_by):
        used = int((sizes > 0).sum())
        fixed = max(1, used // 4)
        shifted = fixed + (places - fixed + offset_by * (used - fixed)) % max(1, number_of - fixed)
        return jnp.zeros((number_of,), jnp.int32).at[order[jnp.where(places < fixed, places, shifted)]].set(jnp.asarray(sizes, jnp.int32))

    sizes = jnp.where(number % 4 == 0, named(heavy_load, number // 4), named(ordinary, number - number // 4 - 1))
    mixed = jax.random.permutation(jax.random.fold_in(own, 3), number_of)
    source_of, receiver = mixed[0:number_of // 2 * 2:2], mixed[1:number_of // 2 * 2:2]
    slack = jnp.minimum(sizes[source_of] - 1, bound - sizes[receiver]) // 2
    slack = jnp.where((source_of == order[0]) | (receiver == order[0]) | (sizes[receiver] == 0), 0, jnp.maximum(slack, 0))
    shifted = jax.random.randint(jax.random.fold_in(own, 4), (number_of // 2,), 0, 1 << 20) % (slack + 1)
    sizes = sizes.at[source_of].add(-shifted).at[receiver].add(shifted)
    labels = jnp.searchsorted(jnp.cumsum(sizes), jnp.arange(rows * top), side="right").astype(jnp.int32)
    listing = labels.reshape(top, rows).T
    listing = listing[jax.random.permutation(jax.random.fold_in(own, 1), rows)]
    offset_by = jax.random.randint(jax.random.fold_in(own, 2), (rows, 1), 0, top)
    return jnp.take_along_axis(listing, (jnp.arange(top)[None, :] + offset_by) % top, axis=1)


def load_shares(count, total, limit, skew, full):
    loads = [(1 << 20) // math.isqrt(grade ** skew) + 1 for grade in range(1, count + 1)]
    largest = limit if full else min(limit, max(-(-total // count), total * loads[0] // sum(loads)))
    least = 1 if total - largest >= count - 1 else 0
    given, rest = [largest] + [least] * (count - 1), total - largest - least * (count - 1)
    while rest > 0:
        free = [i for i in range(1, count) if given[i] < largest] or [i for i in range(1, count) if given[i] < limit]
        mass, left = sum([loads[i] for i in free]), rest
        for i in free:
            addition = min(limit - given[i], max(1, left * loads[i] // mass), rest)
            given[i] = given[i] + addition
            rest = rest - addition
    return np.array(given)


def bell_draw(key, shape, width, limit, split=(), kind=jnp.bfloat16):
    gain = block_scale(key, shape, split, -0.22, 0.18) if split else 1.0
    values = jax.random.normal(key, shape, jnp.float32) * width * gain
    return jnp.minimum(jnp.maximum(values, -limit), limit).astype(kind)


def setup_inputs(seed: int = 0) -> dict:
    key_list = jax.random.split(jax.random.key(seed), 9)
    measures = bell_draw(key_list[0], (TOTAL_ROWS, F), 1.0, 6.0, ((0, 32),))
    pred_columns = with_ends(jax.random.randint(key_list[1], (NPRED, TOTAL_ROWS), 0, 100), jax.random.fold_in(key_list[1], 1), 0, 99).astype(jnp.int32)
    bounds = draw_bounds(jax.random.fold_in(key_list[8], 71), 0)
    lengths = with_ends(jax.random.randint(key_list[3], (TOTAL_ROWS // BLOCK,), BLOCK - 8, BLOCK + 1), jax.random.fold_in(key_list[3], 1), BLOCK - 8, BLOCK).astype(jnp.int32)
    destination_keys = jax.random.split(jax.random.fold_in(key_list[4], 1), TOTAL_ROWS // ROWS_DEV)
    destination_turns = jax.random.permutation(jax.random.fold_in(key_list[4], 3), TOTAL_ROWS // ROWS_DEV)
    destination = jax.vmap(lambda own, number: assign_block(jax.random.fold_in(key_list[4], 2), own, number, ROWS_DEV, DEVICES, 1, CAP, 2))(destination_keys, destination_turns).reshape((TOTAL_ROWS, 1))
    key_offset = with_ends(jax.random.randint(key_list[5], (TOTAL_ROWS,), 0, BUILD_DEV), jax.random.fold_in(key_list[5], 1), 0, BUILD_DEV - 1).astype(jnp.int32)
    group_ids = with_ends(jax.random.randint(key_list[6], (TOTAL_ROWS,), 0, GROUPS), jax.random.fold_in(key_list[6], 1), 0, GROUPS - 1).astype(jnp.int32)
    build_table = bell_draw(key_list[7], (KEYS, F), 1.0, 6.0, ((0, 32),))
    return dict(measures=measures, pred_columns=pred_columns, bounds=bounds, lengths=lengths, destination=destination, key_offset=key_offset, group_ids=group_ids, build_table=build_table)


def reference(measures, pred_columns, bounds, lengths, destination, key_offset, group_ids, build_table):
    total_rows = measures.shape[0]
    within = (lengths[:, None] > jnp.arange(BLOCK, dtype=jnp.int32)[None, :]).reshape(total_rows)
    passes = jnp.all((pred_columns >= bounds[:, 0:1]) & (pred_columns < bounds[:, 1:2]), axis=0)
    usable = within & passes
    join_keys = (destination[:, 0] * BUILD_DEV + key_offset).astype(jnp.int32)
    attributes = jnp.take(build_table, join_keys, axis=0)
    joined = measures.astype(jnp.float32) * attributes.astype(jnp.float32)
    joined = jnp.where(usable[:, None], joined, jnp.zeros_like(joined)).astype(jnp.bfloat16)
    group_sums = jax.ops.segment_sum(joined.astype(jnp.float32), group_ids, num_segments=GROUPS)
    scores = jnp.mean(group_sums, axis=1)
    top_scores = lax.top_k(scores, TOPK)[0]
    return group_sums, top_scores
```

```python
import functools

import jax
import jax.numpy as jnp
from jax import lax
from jax.experimental import pallas as pl
from jax.experimental.pallas import tpu as pltpu
from jax.sharding import PartitionSpec as P

BLOCK = 128
TOPK = 16
GRP_DEV = 32
STRIDE = 11
LOW = 256
MESH = pl.DeviceIdType.MESH
F32 = jnp.float32
BF16 = jnp.bfloat16


def iota(shape, dim, dtype=jnp.int32):
    return lax.broadcasted_iota(jnp.int32, shape, dim).astype(dtype)


def one_hot(condition, dtype=BF16):
    return jnp.where(condition, jnp.ones((), F32), jnp.zeros((), F32)).astype(dtype)


def kernel(
    devices,
    inner,
    cap,
    bounds_ref,
    lengths_ref,
    x_ref,
    pred_ref,
    dest_ref,
    key_ref,
    group_ref,
    table_ref,
    sums_ref,
    top_ref,
    onehot,
    dest_wide,
    masked_meta,
    meta_tiles,
    table_wide,
    send_buf,
    recv_buf,
    acc,
    acc_send,
    part_recv,
    score_send,
    score_recv,
    send_sem,
    recv_sem,
    part_send_sem,
    part_recv_sem,
    score_send_sem,
    score_recv_sem,
):
    rows, width = x_ref.shape
    blocks = rows // BLOCK
    parts = cap // BLOCK
    groups = acc.shape[0]
    high = table_ref.shape[0] // LOW
    me = lax.axis_index("section") * inner + lax.axis_index("dom")

    def partner(step):
        return lax.rem(me + STRIDE * step, devices)

    def address(index):
        return (lax.div(index, inner), lax.rem(index, inner))

    barrier = pltpu.get_barrier_semaphore()

    @pl.loop(1, devices)
    def _(step):
        pl.semaphore_signal(
            barrier, inc=1, device_id=address(partner(step)), device_id_type=MESH
        )

    names = iota((devices, BLOCK), 0)
    matches = [
        (dest_ref[b : b + 1, :] == names).astype(F32) for b in range(blocks)
    ]
    stacked = jnp.concatenate(matches, axis=0).astype(BF16)
    upto = one_hot(iota((BLOCK, BLOCK), 0) <= iota((BLOCK, BLOCK), 1))
    adders = jnp.concatenate([upto, jnp.ones((BLOCK, BLOCK), BF16)], axis=1)
    counts = jnp.dot(stacked, adders, preferred_element_type=F32)
    before = jnp.zeros((devices, BLOCK), F32)
    slots = iota((cap, BLOCK), 0, F32)
    lane = iota((1, BLOCK), 1)
    diagonal = iota((BLOCK, BLOCK), 0) == iota((BLOCK, BLOCK), 1)
    ones = jnp.ones((BLOCK, BLOCK), BF16)
    for b in range(blocks):
        part = counts[b * devices : (b + 1) * devices]
        place = (
            jnp.sum(matches[b] * (part[:, :BLOCK] + before), axis=0, keepdims=True) - 1.0
        )
        before = before + part[:, BLOCK:]
        columns = slice(b * BLOCK, (b + 1) * BLOCK)
        usable = lane < lengths_ref[b]
        for c in range(pred_ref.shape[0]):
            values = pred_ref[c : c + 1, columns]
            usable = usable & (values >= bounds_ref[c, 0]) & (values < bounds_ref[c, 1])
        place = jnp.where(usable, place, -1.0)
        onehot[:, columns] = one_hot(slots == place)
        dest_row = dest_ref[b : b + 1, :].astype(F32)
        dest_diag = jnp.where(diagonal, dest_row, 0.0).astype(BF16)
        dest_wide[columns, :] = jnp.dot(
            dest_diag, ones, preferred_element_type=F32
        ).astype(BF16)
        key = key_ref[b : b + 1, :]
        group = group_ref[b : b + 1, :]
        row8 = iota((16, BLOCK), 0) % 8
        meta = jnp.where(row8 == 0, key // LOW, 0)
        meta = jnp.where(row8 == 1, key % LOW, meta)
        meta = jnp.where(row8 == 2, group // 64, meta)
        meta = jnp.where(row8 == 3, group % 64, meta).astype(F32)
        pair = iota((16, BLOCK), 0) // 8
        for d in range(0, devices, 2):
            masked_meta[d * 8 : d * 8 + 16, columns] = jnp.where(
                dest_ref[b : b + 1, :] == pair + d, meta, 0.0
            ).astype(BF16)
    meta_all = lax.dot_general(
        masked_meta[...], onehot[...], (((1,), (1,)), ((), ())), preferred_element_type=F32
    )
    meta_rows = meta_tiles.shape[1]
    for d in range(devices):
        tiles = [
            meta_all[d * 8 : d * 8 + 8, p * BLOCK : (p + 1) * BLOCK] for p in range(parts)
        ]
        if parts * 8 < meta_rows:
            tiles.append(jnp.zeros((meta_rows - parts * 8, BLOCK), F32))
        meta_tiles[d] = jnp.concatenate(tiles, axis=0).astype(BF16)
    for h in range(high):
        table_wide[:, h * width : (h + 1) * width] = table_ref[h * LOW : (h + 1) * LOW, :]

    pl.semaphore_wait(barrier, devices - 1)

    def row_copy(step):
        return pltpu.make_async_remote_copy(
            src_ref=send_buf.at[step],
            dst_ref=recv_buf.at[step],
            send_sem=send_sem.at[step],
            recv_sem=recv_sem.at[step],
            device_id=address(partner(step)),
            device_id_type=MESH,
        )

    @pl.loop(0, devices // 2)
    def _(index):
        first = 2 * index + 1
        second = lax.rem(first + 1, devices)
        wide = dest_wide[...]
        sides = []
        for step in (first, second):
            name = partner(step).astype(F32).astype(BF16)
            sides.append(jnp.where(wide == name, x_ref[...], jnp.zeros((), BF16)))
        placed = jnp.dot(
            onehot[...], jnp.concatenate(sides, axis=1), preferred_element_type=F32
        ).astype(BF16)
        for at, step in enumerate((first, second)):
            send_buf[step, 0:cap, :] = placed[:, at * width : (at + 1) * width]
            send_buf[step, cap:, :] = meta_tiles[partner(step)]
        row_copy(first).start()

        @pl.when(second > 0)
        def _():
            row_copy(second).start()

    def join_block(buf, step, started):
        payload = buf[step, 0:cap, :].astype(F32)
        tile = buf[step, cap:, :]
        across = tile.astype(F32)
        down = lax.dot_general(
            one_hot(diagonal), tile, (((1,), (1,)), ((), ())), preferred_element_type=F32
        )
        key_high = jnp.concatenate([down[:, 8 * p : 8 * p + 1] for p in range(parts)], axis=0)
        key_low = jnp.concatenate(
            [down[:, 8 * p + 1 : 8 * p + 2] for p in range(parts)], axis=0
        )
        group = jnp.concatenate(
            [
                across[8 * p + 2 : 8 * p + 3] * 64.0 + across[8 * p + 3 : 8 * p + 4]
                for p in range(parts)
            ],
            axis=1,
        )
        picker = one_hot(iota((cap, LOW), 1, F32) == key_low)
        options = jnp.dot(picker, table_wide[...], preferred_element_type=F32)
        fetched = jnp.zeros((cap, width), F32)
        wide_high = jnp.broadcast_to(key_high, (cap, width))
        for h in range(high):
            fetched = jnp.where(
                wide_high == float(h), options[:, h * width : (h + 1) * width], fetched
            )
        joined = (payload * fetched).astype(BF16)
        picker = one_hot(iota((groups, cap), 0, F32) == group)
        terms = jnp.dot(picker, joined, preferred_element_type=F32)
        if started:
            acc[...] += terms
        else:
            acc[...] = terms

    join_block(send_buf, 0, False)

    @pl.loop(1, devices)
    def _(step):
        row_copy(step).wait_recv()
        join_block(recv_buf, step, True)

    acc_send[...] = acc[...].astype(BF16)

    def part_copy(step):
        to = partner(step)
        return pltpu.make_async_remote_copy(
            src_ref=acc_send.at[pl.ds(pl.multiple_of(to * GRP_DEV, GRP_DEV), GRP_DEV)],
            dst_ref=part_recv.at[step],
            send_sem=part_send_sem.at[step],
            recv_sem=part_recv_sem.at[step],
            device_id=address(to),
            device_id_type=MESH,
        )

    @pl.loop(1, devices)
    def _(step):
        part_copy(step).start()

    sums_ref[...] = acc[pl.ds(pl.multiple_of(me * GRP_DEV, GRP_DEV), GRP_DEV), :]

    @pl.loop(1, devices)
    def _(step):
        row_copy(step).wait_send()

    @pl.loop(1, devices)
    def _(step):
        part_copy(step).wait_recv()
        sums_ref[...] += part_recv[step].astype(F32)

    score = jnp.sum(sums_ref[...], axis=1, keepdims=True) / width
    spot = (GRP_DEV, BLOCK)
    across = jnp.sum(
        jnp.where(iota(spot, 0) == iota(spot, 1), score, 0.0), axis=0, keepdims=True
    )
    across = jnp.where(lane < GRP_DEV, across, -jnp.inf)
    score_send[...] = jnp.broadcast_to(across, score_send.shape)
    score_recv[0] = score_send[...]

    def score_copy(step):
        return pltpu.make_async_remote_copy(
            src_ref=score_send,
            dst_ref=score_recv.at[step],
            send_sem=score_send_sem.at[step],
            recv_sem=score_recv_sem.at[step],
            device_id=address(partner(step)),
            device_id_type=MESH,
        )

    @pl.loop(1, devices)
    def _(step):
        score_copy(step).start()

    @pl.loop(1, devices)
    def _(step):
        part_copy(step).wait_send()

    @pl.loop(1, devices)
    def _(step):
        score_copy(step).wait_recv()

    scores = score_recv[:, 0, :]
    spots = iota((1, BLOCK), 1, F32)
    top = jnp.zeros((1, BLOCK), F32)
    filled = jnp.zeros((1, 1), F32)
    limit = None
    for _ in range(TOPK):
        left = scores if limit is None else jnp.where(scores < limit, scores, -jnp.inf)
        limit = jnp.max(jnp.max(left, axis=0, keepdims=True), axis=1, keepdims=True)
        top = jnp.where(spots >= filled, limit, top)
        same = jnp.where(scores == limit, 1.0, 0.0)
        filled = filled + jnp.sum(
            jnp.sum(same, axis=0, keepdims=True), axis=1, keepdims=True
        )
    top_ref[...] = top

    @pl.loop(1, devices)
    def _(step):
        score_copy(step).wait_send()


def on_device(
    devices,
    inner,
    measures,
    pred_columns,
    bounds,
    lengths,
    destination,
    key_offset,
    group_ids,
    build_table,
):
    rows, width = measures.shape
    blocks = rows // BLOCK
    cap = max(BLOCK, 2 * rows // devices)
    parts = cap // BLOCK
    meta_rows = 16 * ((parts * 8 + 15) // 16)
    slot_rows = cap + meta_rows
    groups = GRP_DEV * devices
    vmem = pl.BlockSpec(memory_space=pltpu.VMEM)
    smem = pl.BlockSpec(memory_space=pltpu.SMEM)
    sums, top = pl.pallas_call(
        functools.partial(kernel, devices, inner, cap),
        out_shape=(
            jax.ShapeDtypeStruct((GRP_DEV, width), F32),
            jax.ShapeDtypeStruct((1, BLOCK), F32),
        ),
        in_specs=[smem, smem] + [vmem] * 6,
        out_specs=(vmem, vmem),
        scratch_shapes=[
            pltpu.VMEM((cap, rows), BF16),
            pltpu.VMEM((rows, width), BF16),
            pltpu.VMEM((devices * 8, rows), BF16),
            pltpu.VMEM((devices, meta_rows, BLOCK), BF16),
            pltpu.VMEM((LOW, build_table.shape[0] // LOW * width), BF16),
            pltpu.VMEM((devices, slot_rows, width), BF16),
            pltpu.VMEM((devices, slot_rows, width), BF16),
            pltpu.VMEM((groups, width), F32),
            pltpu.VMEM((groups, width), BF16),
            pltpu.VMEM((devices, GRP_DEV, width), BF16),
            pltpu.VMEM((8, BLOCK), F32),
            pltpu.VMEM((devices, 8, BLOCK), F32),
        ]
        + [pltpu.SemaphoreType.DMA((devices,))] * 6,
        compiler_params=pltpu.CompilerParams(
            collective_id=0, has_side_effects=True, vmem_limit_bytes=56 * 1024 * 1024
        ),
    )(
        bounds,
        lengths,
        measures,
        pred_columns,
        destination.reshape(blocks, BLOCK),
        key_offset.reshape(blocks, BLOCK),
        group_ids.reshape(blocks, BLOCK),
        build_table,
    )
    return (sums, top[0, :TOPK])


def solution(mesh):
    both = ("section", "dom")
    inner = mesh.shape["dom"]
    devices = mesh.shape["section"] * inner
    return jax.shard_map(
        functools.partial(on_device, devices, inner),
        mesh=mesh,
        in_specs=(
            P(both, None),
            P(None, both),
            P(),
            P(both),
            P(both, None),
            P(both),
            P(both),
            P(both, None),
        ),
        out_specs=(P(both, None), P()),
        check_vma=False,
    )
```

```python
import functools

import jax
import jax.numpy as jnp
from jax import lax
from jax.experimental import pallas as pl
from jax.experimental.pallas import tpu as pltpu
from jax.sharding import PartitionSpec as P

BLOCK = 128
TOPK = 16
GRP_DEV = 32
STRIDE = 11
LOW = 256
CORES = 2
MESH = pl.DeviceIdType.MESH
F32 = jnp.float32
BF16 = jnp.bfloat16


def iota(shape, dim, dtype=jnp.int32):
    return lax.broadcasted_iota(jnp.int32, shape, dim).astype(dtype)


def one_hot(condition, dtype=BF16):
    return jnp.where(condition, jnp.ones((), F32), jnp.zeros((), F32)).astype(dtype)


def kernel(
    devices,
    inner,
    cap,
    bounds_ref,
    lengths_ref,
    x_ref,
    pred_ref,
    dest_ref,
    key_ref,
    group_ref,
    table_ref,
    sums_ref,
    top_ref,
    onehot,
    dest_wide,
    masked_meta,
    meta_tiles,
    table_wide,
    send_buf,
    recv_buf,
    acc,
    acc_send,
    part_recv,
    score_send,
    score_recv,
    shards,
    shard_send_sem,
    shard_recv_sem,
    send_sem,
    recv_sem,
    part_send_sem,
    part_recv_sem,
    score_send_sem,
    score_recv_sem,
):
    rows, width = x_ref.shape
    blocks = rows // BLOCK
    parts = cap // BLOCK
    groups = acc.shape[0]
    high = table_ref.shape[0] // LOW
    me = lax.axis_index("section") * inner + lax.axis_index("dom")

    def partner(step):
        return lax.rem(me + STRIDE * step, devices)

    def address(index):
        return (lax.div(index, inner), lax.rem(index, inner))

    barrier = pltpu.get_barrier_semaphore()

    @pl.loop(1, devices)
    def _(step):
        pl.semaphore_signal(
            barrier, inc=1, device_id=address(partner(step)), device_id_type=MESH
        )

    sections = devices // inner
    depth = inner // CORES
    peers = sections * CORES
    section = lax.axis_index("section")
    level = lax.div(lax.axis_index("dom"), CORES)
    core = lax.rem(lax.axis_index("dom"), CORES)

    def shard_copy(source, shard, way):
        return pltpu.make_async_remote_copy(
            src_ref=source,
            dst_ref=shards.at[shard],
            send_sem=shard_send_sem.at[way, shard],
            recv_sem=shard_recv_sem.at[shard],
            device_id=(
                section,
                lax.rem(level + 1 + way * (depth - 2), depth) * CORES + core,
            ),
            device_id_type=MESH,
        )

    def shard_round(distance):
        below = level - distance
        above = level + distance

        @pl.when(below >= 0)
        def _():
            shard_copy(shards.at[below], below, 0).wait_recv()

            @pl.when(level + 1 < depth)
            def _():
                shard_copy(shards.at[below], below, 0).start()

        @pl.when(above < depth)
        def _():
            shard_copy(shards.at[above], above, 1).wait_recv()

            @pl.when(level > 0)
            def _():
                shard_copy(shards.at[above], above, 1).start()

    def level_at(place):
        far = lax.div(place + 1, 2)
        near = jnp.where(lax.rem(place, 2) == 1, level - far, level + far)
        upper = depth - 1 - level
        rest = jnp.where(level < upper, place, depth - 1 - place)
        return jnp.where(place <= 2 * jnp.minimum(level, upper), near, rest)

    pl.semaphore_wait(barrier, devices - 1)

    @pl.when(level + 1 < depth)
    def _():
        shard_copy(table_ref, level, 0).start()

    @pl.when(level > 0)
    def _():
        shard_copy(table_ref, level, 1).start()

    acc[...] = jnp.zeros_like(acc)

    names = iota((devices, BLOCK), 0)
    matches = [
        (dest_ref[b : b + 1, :] == names).astype(F32) for b in range(blocks)
    ]
    stacked = jnp.concatenate(matches, axis=0).astype(BF16)
    upto = one_hot(iota((BLOCK, BLOCK), 0) <= iota((BLOCK, BLOCK), 1))
    adders = jnp.concatenate([upto, jnp.ones((BLOCK, BLOCK), BF16)], axis=1)
    counts = jnp.dot(stacked, adders, preferred_element_type=F32)
    before = jnp.zeros((devices, BLOCK), F32)
    slots = iota((cap, BLOCK), 0, F32)
    lane = iota((1, BLOCK), 1)
    diagonal = iota((BLOCK, BLOCK), 0) == iota((BLOCK, BLOCK), 1)
    ones = jnp.ones((BLOCK, BLOCK), BF16)
    for b in range(blocks):
        part = counts[b * devices : (b + 1) * devices]
        place = (
            jnp.sum(matches[b] * (part[:, :BLOCK] + before), axis=0, keepdims=True) - 1.0
        )
        before = before + part[:, BLOCK:]
        columns = slice(b * BLOCK, (b + 1) * BLOCK)
        usable = lane < lengths_ref[b]
        for c in range(pred_ref.shape[0]):
            values = pred_ref[c : c + 1, columns]
            usable = usable & (values >= bounds_ref[c, 0]) & (values < bounds_ref[c, 1])
        place = jnp.where(usable, place, -1.0)
        onehot[:, columns] = one_hot(slots == place)
        dest_row = dest_ref[b : b + 1, :].astype(F32)
        dest_diag = jnp.where(diagonal, dest_row, 0.0).astype(BF16)
        dest_wide[columns, :] = jnp.dot(
            dest_diag, ones, preferred_element_type=F32
        ).astype(BF16)
        key = key_ref[b : b + 1, :]
        group = group_ref[b : b + 1, :]
        row8 = iota((16, BLOCK), 0) % 8
        meta = jnp.where(row8 == 0, key // LOW, 0)
        meta = jnp.where(row8 == 1, key % LOW, meta)
        meta = jnp.where(row8 == 2, group // 64, meta)
        meta = jnp.where(row8 == 3, group % 64, meta).astype(F32)
        pair = iota((16, BLOCK), 0) // 8
        for d in range(0, devices, 2):
            masked_meta[d * 8 : d * 8 + 16, columns] = jnp.where(
                dest_ref[b : b + 1, :] == pair + d, meta, 0.0
            ).astype(BF16)
    meta_all = lax.dot_general(
        masked_meta[...], onehot[...], (((1,), (1,)), ((), ())), preferred_element_type=F32
    )
    meta_rows = meta_tiles.shape[1]
    for d in range(devices):
        tiles = [
            meta_all[d * 8 : d * 8 + 8, p * BLOCK : (p + 1) * BLOCK] for p in range(parts)
        ]
        if parts * 8 < meta_rows:
            tiles.append(jnp.zeros((meta_rows - parts * 8, BLOCK), F32))
        meta_tiles[d] = jnp.concatenate(tiles, axis=0).astype(BF16)
    def target(offset):
        to = lax.rem(section + lax.div(offset, CORES), sections)
        return to, lax.rem(core + lax.rem(offset, CORES), CORES)

    def row_copy(slot, offset):
        to, to_core = target(offset)
        return pltpu.make_async_remote_copy(
            src_ref=send_buf.at[slot],
            dst_ref=recv_buf.at[slot],
            send_sem=send_sem.at[slot],
            recv_sem=recv_sem.at[slot],
            device_id=(to, level * CORES + to_core),
            device_id_type=MESH,
        )

    def send_rows(place):
        owner_level = level_at(place)

        @pl.loop(0, peers // 2)
        def _(index):
            base = peers - 2 - 2 * index
            owners = []
            for offset in (base, base + 1):
                to, to_core = target(offset)
                owners.append(to * inner + owner_level * CORES + to_core)
            wide = dest_wide[...]
            sides = []
            for owner in owners:
                name = owner.astype(F32).astype(BF16)
                sides.append(jnp.where(wide == name, x_ref[...], jnp.zeros((), BF16)))
            placed = jnp.dot(
                onehot[...], jnp.concatenate(sides, axis=1), preferred_element_type=F32
            ).astype(BF16)
            for at, owner in enumerate(owners):
                slot = owner_level * peers + base + at
                send_buf[slot, 0:cap, :] = placed[:, at * width : (at + 1) * width]
                send_buf[slot, cap:, :] = meta_tiles[owner]
            slot = owner_level * peers + base
            row_copy(slot + 1, base + 1).start()

            @pl.when(base > 0)
            def _():
                row_copy(slot, base).start()

            @pl.when(base == 0)
            def _():
                recv_buf[slot] = send_buf[slot]

    def join_block(buf, step):
        payload = buf[step, 0:cap, :].astype(F32)
        tile = buf[step, cap:, :]
        across = tile.astype(F32)
        down = lax.dot_general(
            one_hot(diagonal), tile, (((1,), (1,)), ((), ())), preferred_element_type=F32
        )
        key_high = jnp.concatenate([down[:, 8 * p : 8 * p + 1] for p in range(parts)], axis=0)
        key_low = jnp.concatenate(
            [down[:, 8 * p + 1 : 8 * p + 2] for p in range(parts)], axis=0
        )
        group = jnp.concatenate(
            [
                across[8 * p + 2 : 8 * p + 3] * 64.0 + across[8 * p + 3 : 8 * p + 4]
                for p in range(parts)
            ],
            axis=1,
        )
        picker = one_hot(iota((cap, LOW), 1, F32) == key_low)
        options = jnp.dot(picker, table_wide[...], preferred_element_type=F32)
        fetched = jnp.zeros((cap, width), F32)
        wide_high = jnp.broadcast_to(key_high, (cap, width))
        for h in range(high):
            fetched = jnp.where(
                wide_high == float(h), options[:, h * width : (h + 1) * width], fetched
            )
        joined = (payload * fetched).astype(BF16)
        picker = one_hot(iota((groups, cap), 0, F32) == group)
        terms = jnp.dot(picker, joined, preferred_element_type=F32)
        acc[...] += terms

    def widen(source):
        for h in range(high):
            table_wide[:, h * width : (h + 1) * width] = source[h * LOW : (h + 1) * LOW, :]

    early = min(2, depth)

    @pl.loop(0, early)
    def _(place):
        send_rows(place)

    if depth > 1:
        shard_round(1)

    @pl.loop(early, depth)
    def _(place):
        send_rows(place)

    @pl.loop(0, depth)
    def _(place):
        if depth > 2:

            @pl.when((place >= 1) & (place + 1 < depth - 1))
            def _():
                shard_round(place + 1)

            @pl.when(place == depth - 1)
            def _():
                shard_round(depth - 1)

        owner_level = level_at(place)

        @pl.when(place == 0)
        def _():
            widen(table_ref)

        @pl.when(place > 0)
        def _():
            widen(shards.at[owner_level])

        @pl.loop(0, peers)
        def _(offset):
            slot = owner_level * peers + offset

            @pl.when(offset > 0)
            def _():
                row_copy(slot, offset).wait_recv()

            join_block(recv_buf, slot)

    acc_send[...] = acc[...].astype(BF16)

    def part_copy(step):
        to = partner(step)
        return pltpu.make_async_remote_copy(
            src_ref=acc_send.at[pl.ds(pl.multiple_of(to * GRP_DEV, GRP_DEV), GRP_DEV)],
            dst_ref=part_recv.at[step],
            send_sem=part_send_sem.at[step],
            recv_sem=part_recv_sem.at[step],
            device_id=address(to),
            device_id_type=MESH,
        )

    @pl.loop(1, devices)
    def _(step):
        part_copy(step).start()

    sums_ref[...] = acc[pl.ds(pl.multiple_of(me * GRP_DEV, GRP_DEV), GRP_DEV), :]

    @pl.loop(0, depth)
    def _(at):
        @pl.loop(1, peers)
        def _(offset):
            row_copy(at * peers + offset, offset).wait_send()

        @pl.when((at <= level) & (level + 1 < depth))
        def _():
            shard_copy(shards.at[at], at, 0).wait_send()

        @pl.when((at >= level) & (level > 0))
        def _():
            shard_copy(shards.at[at], at, 1).wait_send()

    @pl.loop(1, devices)
    def _(step):
        part_copy(step).wait_recv()
        sums_ref[...] += part_recv[step].astype(F32)

    score = jnp.sum(sums_ref[...], axis=1, keepdims=True) / width
    spot = (GRP_DEV, BLOCK)
    across = jnp.sum(
        jnp.where(iota(spot, 0) == iota(spot, 1), score, 0.0), axis=0, keepdims=True
    )
    across = jnp.where(lane < GRP_DEV, across, -jnp.inf)
    score_send[...] = jnp.broadcast_to(across, score_send.shape)
    score_recv[0] = score_send[...]

    def score_copy(step):
        return pltpu.make_async_remote_copy(
            src_ref=score_send,
            dst_ref=score_recv.at[step],
            send_sem=score_send_sem.at[step],
            recv_sem=score_recv_sem.at[step],
            device_id=address(partner(step)),
            device_id_type=MESH,
        )

    @pl.loop(1, devices)
    def _(step):
        score_copy(step).start()

    @pl.loop(1, devices)
    def _(step):
        part_copy(step).wait_send()

    @pl.loop(1, devices)
    def _(step):
        score_copy(step).wait_recv()

    scores = score_recv[:, 0, :]
    spots = iota((1, BLOCK), 1, F32)
    top = jnp.zeros((1, BLOCK), F32)
    filled = jnp.zeros((1, 1), F32)
    limit = None
    for _ in range(TOPK):
        left = scores if limit is None else jnp.where(scores < limit, scores, -jnp.inf)
        limit = jnp.max(jnp.max(left, axis=0, keepdims=True), axis=1, keepdims=True)
        top = jnp.where(spots >= filled, limit, top)
        same = jnp.where(scores == limit, 1.0, 0.0)
        filled = filled + jnp.sum(
            jnp.sum(same, axis=0, keepdims=True), axis=1, keepdims=True
        )
    top_ref[...] = top

    @pl.loop(1, devices)
    def _(step):
        score_copy(step).wait_send()


def on_device(
    devices,
    inner,
    measures,
    pred_columns,
    bounds,
    lengths,
    destination,
    key_offset,
    group_ids,
    build_table,
):
    rows, width = measures.shape
    blocks = rows // BLOCK
    cap = max(BLOCK, 2 * rows // devices)
    parts = cap // BLOCK
    meta_rows = 16 * ((parts * 8 + 15) // 16)
    slot_rows = cap + meta_rows
    groups = GRP_DEV * devices
    vmem = pl.BlockSpec(memory_space=pltpu.VMEM)
    smem = pl.BlockSpec(memory_space=pltpu.SMEM)
    sums, top = pl.pallas_call(
        functools.partial(kernel, devices, inner, cap),
        out_shape=(
            jax.ShapeDtypeStruct((GRP_DEV, width), F32),
            jax.ShapeDtypeStruct((1, BLOCK), F32),
        ),
        in_specs=[smem, smem] + [vmem] * 6,
        out_specs=(vmem, vmem),
        scratch_shapes=[
            pltpu.VMEM((cap, rows), BF16),
            pltpu.VMEM((rows, width), BF16),
            pltpu.VMEM((devices * 8, rows), BF16),
            pltpu.VMEM((devices, meta_rows, BLOCK), BF16),
            pltpu.VMEM((LOW, build_table.shape[0] // LOW * width), BF16),
            pltpu.VMEM((devices, slot_rows, width), BF16),
            pltpu.VMEM((devices, slot_rows, width), BF16),
            pltpu.VMEM((groups, width), F32),
            pltpu.VMEM((groups, width), BF16),
            pltpu.VMEM((devices, GRP_DEV, width), BF16),
            pltpu.VMEM((8, BLOCK), F32),
            pltpu.VMEM((devices, 8, BLOCK), F32),
            pltpu.VMEM((inner // CORES,) + build_table.shape, BF16),
            pltpu.SemaphoreType.DMA((2, inner // CORES)),
            pltpu.SemaphoreType.DMA((inner // CORES,)),
        ]
        + [pltpu.SemaphoreType.DMA((devices,))] * 6,
        compiler_params=pltpu.CompilerParams(
            collective_id=0, has_side_effects=True, vmem_limit_bytes=56 * 1024 * 1024
        ),
    )(
        bounds,
        lengths,
        measures,
        pred_columns,
        destination.reshape(blocks, BLOCK),
        key_offset.reshape(blocks, BLOCK),
        group_ids.reshape(blocks, BLOCK),
        build_table,
    )
    return (sums, top[0, :TOPK])


def solution(mesh):
    both = ("section", "dom")
    inner = mesh.shape["dom"]
    devices = mesh.shape["section"] * inner
    return jax.shard_map(
        functools.partial(on_device, devices, inner),
        mesh=mesh,
        in_specs=(
            P(both, None),
            P(None, both),
            P(),
            P(both),
            P(both, None),
            P(both),
            P(both),
            P(both, None),
        ),
        out_specs=(P(both, None), P()),
        check_vma=False,
    )
```

```python
import functools

import jax
import jax.numpy as jnp
from jax import lax
from jax.experimental import pallas as pl
from jax.experimental.pallas import tpu as pltpu
from jax.sharding import PartitionSpec as P

BLOCK = 128
TOPK = 16
GRP_DEV = 32
STRIDE = 11
LOW = 256
CORES = 2
MESH = pl.DeviceIdType.MESH
F32 = jnp.float32
BF16 = jnp.bfloat16


def iota(shape, dim, dtype=jnp.int32):
    return lax.broadcasted_iota(jnp.int32, shape, dim).astype(dtype)


def one_hot(condition, dtype=BF16):
    return jnp.where(condition, jnp.ones((), F32), jnp.zeros((), F32)).astype(dtype)


def kernel(
    devices,
    inner,
    cap,
    bounds_ref,
    lengths_ref,
    x_ref,
    pred_ref,
    dest_ref,
    key_ref,
    group_ref,
    table_ref,
    sums_ref,
    top_ref,
    onehot,
    spread,
    inner_wide,
    masked_meta,
    meta_tiles,
    table_wide,
    send_buf,
    recv_buf,
    acc,
    acc_send,
    part_recv,
    score_send,
    score_recv,
    shards,
    shard_send_sem,
    shard_recv_sem,
    send_sem,
    recv_sem,
    part_send_sem,
    part_recv_sem,
    score_send_sem,
    score_recv_sem,
):
    rows, width = x_ref.shape
    blocks = rows // BLOCK
    parts = cap // BLOCK
    groups = acc.shape[0]
    high = table_ref.shape[0] // LOW
    me = lax.axis_index("section") * inner + lax.axis_index("dom")

    def partner(step):
        return lax.rem(me + STRIDE * step, devices)

    def address(index):
        return (lax.div(index, inner), lax.rem(index, inner))

    barrier = pltpu.get_barrier_semaphore()

    @pl.loop(1, devices)
    def _(step):
        pl.semaphore_signal(
            barrier, inc=1, device_id=address(partner(step)), device_id_type=MESH
        )

    sections = devices // inner
    depth = inner // CORES
    peers = sections * CORES
    section = lax.axis_index("section")
    level = lax.div(lax.axis_index("dom"), CORES)
    core = lax.rem(lax.axis_index("dom"), CORES)

    def shard_copy(source, shard, way):
        return pltpu.make_async_remote_copy(
            src_ref=source,
            dst_ref=shards.at[shard],
            send_sem=shard_send_sem.at[way, shard],
            recv_sem=shard_recv_sem.at[shard],
            device_id=(
                section,
                lax.rem(level + 1 + way * (depth - 2), depth) * CORES + core,
            ),
            device_id_type=MESH,
        )

    def shard_round(distance):
        below = level - distance
        above = level + distance

        @pl.when(below >= 0)
        def _():
            shard_copy(shards.at[below], below, 0).wait_recv()

            @pl.when(level + 1 < depth)
            def _():
                shard_copy(shards.at[below], below, 0).start()

        @pl.when(above < depth)
        def _():
            shard_copy(shards.at[above], above, 1).wait_recv()

            @pl.when(level > 0)
            def _():
                shard_copy(shards.at[above], above, 1).start()

    def level_at(place):
        far = lax.div(place + 1, 2)
        near = jnp.where(lax.rem(place, 2) == 1, level - far, level + far)
        upper = depth - 1 - level
        rest = jnp.where(level < upper, place, depth - 1 - place)
        return jnp.where(place <= 2 * jnp.minimum(level, upper), near, rest)

    pl.semaphore_wait(barrier, devices - 1)

    @pl.when(level + 1 < depth)
    def _():
        shard_copy(table_ref, level, 0).start()

    @pl.when(level > 0)
    def _():
        shard_copy(table_ref, level, 1).start()

    acc[...] = jnp.zeros_like(acc)

    names = iota((devices, BLOCK), 0)
    matches = [
        (dest_ref[b : b + 1, :] == names).astype(F32) for b in range(blocks)
    ]
    stacked = jnp.concatenate(matches, axis=0).astype(BF16)
    upto = one_hot(iota((BLOCK, BLOCK), 0) <= iota((BLOCK, BLOCK), 1))
    adders = jnp.concatenate([upto, jnp.ones((BLOCK, BLOCK), BF16)], axis=1)
    counts = jnp.dot(stacked, adders, preferred_element_type=F32)
    before = jnp.zeros((devices, BLOCK), F32)
    slots = iota((cap, BLOCK), 0, F32)
    lane = iota((1, BLOCK), 1)
    diagonal = iota((BLOCK, BLOCK), 0) == iota((BLOCK, BLOCK), 1)
    ones = jnp.ones((BLOCK, BLOCK), BF16)
    spread_slots = iota((sections * cap, BLOCK), 0, F32)
    dest_section = lax.div(dest_ref[...], inner)
    dest_inner = (dest_ref[...] - dest_section * inner).astype(F32)
    section_base = dest_section.astype(F32) * cap
    for b in range(blocks):
        part = counts[b * devices : (b + 1) * devices]
        place = (
            jnp.sum(matches[b] * (part[:, :BLOCK] + before), axis=0, keepdims=True) - 1.0
        )
        before = before + part[:, BLOCK:]
        columns = slice(b * BLOCK, (b + 1) * BLOCK)
        usable = lane < lengths_ref[b]
        for c in range(pred_ref.shape[0]):
            values = pred_ref[c : c + 1, columns]
            usable = usable & (values >= bounds_ref[c, 0]) & (values < bounds_ref[c, 1])
        place = jnp.where(usable, place, -1.0)
        onehot[:, columns] = one_hot(slots == place)
        place = jnp.where(usable, place + section_base[b : b + 1], -1.0)
        spread[:, columns] = one_hot(spread_slots == place)
        inner_diag = jnp.where(diagonal, dest_inner[b : b + 1], 0.0).astype(BF16)
        inner_wide[columns, :] = jnp.dot(
            inner_diag, ones, preferred_element_type=F32
        ).astype(BF16)
        key = key_ref[b : b + 1, :]
        group = group_ref[b : b + 1, :]
        row8 = iota((16, BLOCK), 0) % 8
        meta = jnp.where(row8 == 0, key // LOW, 0)
        meta = jnp.where(row8 == 1, key % LOW, meta)
        meta = jnp.where(row8 == 2, group // 64, meta)
        meta = jnp.where(row8 == 3, group % 64, meta).astype(F32)
        pair = iota((16, BLOCK), 0) // 8
        for d in range(0, devices, 2):
            masked_meta[d * 8 : d * 8 + 16, columns] = jnp.where(
                dest_ref[b : b + 1, :] == pair + d, meta, 0.0
            ).astype(BF16)
    meta_all = lax.dot_general(
        masked_meta[...], onehot[...], (((1,), (1,)), ((), ())), preferred_element_type=F32
    )
    meta_rows = meta_tiles.shape[1]
    for d in range(devices):
        tiles = [
            meta_all[d * 8 : d * 8 + 8, p * BLOCK : (p + 1) * BLOCK] for p in range(parts)
        ]
        if parts * 8 < meta_rows:
            tiles.append(jnp.zeros((meta_rows - parts * 8, BLOCK), F32))
        meta_tiles[d] = jnp.concatenate(tiles, axis=0).astype(BF16)
    def target(offset):
        to = lax.rem(section + lax.div(offset, CORES), sections)
        return to, lax.rem(core + lax.rem(offset, CORES), CORES)

    def row_copy(slot, offset):
        to, to_core = target(offset)
        return pltpu.make_async_remote_copy(
            src_ref=send_buf.at[slot],
            dst_ref=recv_buf.at[slot],
            send_sem=send_sem.at[slot],
            recv_sem=recv_sem.at[slot],
            device_id=(to, level * CORES + to_core),
            device_id_type=MESH,
        )

    def send_rows(place):
        owner_level = level_at(place)
        sides = []
        for c in range(CORES):
            name = (owner_level * CORES + c).astype(F32).astype(BF16)
            sides.append(
                jnp.where(inner_wide[...] == name, x_ref[...], jnp.zeros((), BF16))
            )
        placed = jnp.dot(
            spread[...], jnp.concatenate(sides, axis=1), preferred_element_type=F32
        ).astype(BF16)
        for to in range(sections):
            for c in range(CORES):
                offset = lax.rem(to - section + sections, sections) * CORES + lax.rem(
                    c - core + CORES, CORES
                )
                slot = owner_level * peers + offset
                send_buf[slot, 0:cap, :] = placed[
                    to * cap : (to + 1) * cap, c * width : (c + 1) * width
                ]
                send_buf[slot, cap:, :] = meta_tiles[
                    to * inner + owner_level * CORES + c
                ]

        @pl.loop(1, peers)
        def _(index):
            offset = peers - index
            row_copy(owner_level * peers + offset, offset).start()

        recv_buf[owner_level * peers] = send_buf[owner_level * peers]

    def join_blocks(first, batch):
        payload, key_high, key_low, group = [], [], [], []
        for at in range(batch):
            payload.append(recv_buf[first + at, 0:cap, :])
            tile = recv_buf[first + at, cap:, :]
            across = tile.astype(F32)
            down = lax.dot_general(
                one_hot(diagonal),
                tile,
                (((1,), (1,)), ((), ())),
                preferred_element_type=F32,
            )
            for p in range(parts):
                key_high.append(down[:, 8 * p : 8 * p + 1])
                key_low.append(down[:, 8 * p + 1 : 8 * p + 2])
                group.append(
                    across[8 * p + 2 : 8 * p + 3] * 64.0 + across[8 * p + 3 : 8 * p + 4]
                )
        payload = jnp.concatenate(payload, axis=0).astype(F32)
        key_high = jnp.concatenate(key_high, axis=0)
        key_low = jnp.concatenate(key_low, axis=0)
        group = jnp.concatenate(group, axis=1)
        size = batch * cap
        picker = one_hot(iota((size, LOW), 1, F32) == key_low)
        options = jnp.dot(picker, table_wide[...], preferred_element_type=F32)
        fetched = jnp.zeros((size, width), F32)
        wide_high = jnp.broadcast_to(key_high, (size, width))
        for h in range(high):
            fetched = jnp.where(
                wide_high == float(h), options[:, h * width : (h + 1) * width], fetched
            )
        joined = (payload * fetched).astype(BF16)
        picker = one_hot(iota((groups, size), 0, F32) == group)
        acc[...] += jnp.dot(picker, joined, preferred_element_type=F32)

    def widen(source):
        for h in range(high):
            table_wide[:, h * width : (h + 1) * width] = source[h * LOW : (h + 1) * LOW, :]

    early = min(2, depth)

    @pl.loop(0, early)
    def _(place):
        send_rows(place)

    if depth > 1:
        shard_round(1)

    @pl.loop(early, depth)
    def _(place):
        send_rows(place)

    @pl.loop(0, depth)
    def _(place):
        if depth > 2:

            @pl.when((place >= 1) & (place + 1 < depth - 1))
            def _():
                shard_round(place + 1)

            @pl.when(place == depth - 1)
            def _():
                shard_round(depth - 1)

        owner_level = level_at(place)

        @pl.when(place == 0)
        def _():
            widen(table_ref)

        @pl.when(place > 0)
        def _():
            widen(shards.at[owner_level])

        batch = min(4, peers)

        @pl.loop(0, peers // batch)
        def _(index):
            base = index * batch
            for at in range(batch):
                offset = base + at

                @pl.when(offset > 0)
                def _():
                    row_copy(owner_level * peers + offset, offset).wait_recv()

            join_blocks(owner_level * peers + base, batch)

    acc_send[...] = acc[...].astype(BF16)

    def part_copy(step):
        to = partner(step)
        return pltpu.make_async_remote_copy(
            src_ref=acc_send.at[pl.ds(pl.multiple_of(to * GRP_DEV, GRP_DEV), GRP_DEV)],
            dst_ref=part_recv.at[step],
            send_sem=part_send_sem.at[step],
            recv_sem=part_recv_sem.at[step],
            device_id=address(to),
            device_id_type=MESH,
        )

    @pl.loop(1, devices)
    def _(step):
        part_copy(step).start()

    sums_ref[...] = acc[pl.ds(pl.multiple_of(me * GRP_DEV, GRP_DEV), GRP_DEV), :]

    @pl.loop(0, depth)
    def _(at):
        @pl.loop(1, peers)
        def _(offset):
            row_copy(at * peers + offset, offset).wait_send()

        @pl.when((at <= level) & (level + 1 < depth))
        def _():
            shard_copy(shards.at[at], at, 0).wait_send()

        @pl.when((at >= level) & (level > 0))
        def _():
            shard_copy(shards.at[at], at, 1).wait_send()

    @pl.loop(1, devices)
    def _(step):
        part_copy(step).wait_recv()
        sums_ref[...] += part_recv[step].astype(F32)

    score = jnp.sum(sums_ref[...], axis=1, keepdims=True) / width
    spot = (GRP_DEV, BLOCK)
    across = jnp.sum(
        jnp.where(iota(spot, 0) == iota(spot, 1), score, 0.0), axis=0, keepdims=True
    )
    across = jnp.where(lane < GRP_DEV, across, -jnp.inf)
    score_send[...] = jnp.broadcast_to(across, score_send.shape)
    score_recv[0] = score_send[...]

    def score_copy(step):
        return pltpu.make_async_remote_copy(
            src_ref=score_send,
            dst_ref=score_recv.at[step],
            send_sem=score_send_sem.at[step],
            recv_sem=score_recv_sem.at[step],
            device_id=address(partner(step)),
            device_id_type=MESH,
        )

    @pl.loop(1, devices)
    def _(step):
        score_copy(step).start()

    @pl.loop(1, devices)
    def _(step):
        part_copy(step).wait_send()

    @pl.loop(1, devices)
    def _(step):
        score_copy(step).wait_recv()

    scores = score_recv[:, 0, :]
    spots = iota((1, BLOCK), 1, F32)
    top = jnp.zeros((1, BLOCK), F32)
    filled = jnp.zeros((1, 1), F32)
    limit = None
    for _ in range(TOPK):
        left = scores if limit is None else jnp.where(scores < limit, scores, -jnp.inf)
        limit = jnp.max(jnp.max(left, axis=0, keepdims=True), axis=1, keepdims=True)
        top = jnp.where(spots >= filled, limit, top)
        same = jnp.where(scores == limit, 1.0, 0.0)
        filled = filled + jnp.sum(
            jnp.sum(same, axis=0, keepdims=True), axis=1, keepdims=True
        )
    top_ref[...] = top

    @pl.loop(1, devices)
    def _(step):
        score_copy(step).wait_send()


def on_device(
    devices,
    inner,
    measures,
    pred_columns,
    bounds,
    lengths,
    destination,
    key_offset,
    group_ids,
    build_table,
):
    rows, width = measures.shape
    blocks = rows // BLOCK
    cap = max(BLOCK, 2 * rows // devices)
    parts = cap // BLOCK
    meta_rows = 16 * ((parts * 8 + 15) // 16)
    slot_rows = cap + meta_rows
    groups = GRP_DEV * devices
    vmem = pl.BlockSpec(memory_space=pltpu.VMEM)
    smem = pl.BlockSpec(memory_space=pltpu.SMEM)
    sums, top = pl.pallas_call(
        functools.partial(kernel, devices, inner, cap),
        out_shape=(
            jax.ShapeDtypeStruct((GRP_DEV, width), F32),
            jax.ShapeDtypeStruct((1, BLOCK), F32),
        ),
        in_specs=[smem, smem] + [vmem] * 6,
        out_specs=(vmem, vmem),
        scratch_shapes=[
            pltpu.VMEM((cap, rows), BF16),
            pltpu.VMEM((devices // inner * cap, rows), BF16),
            pltpu.VMEM((rows, width), BF16),
            pltpu.VMEM((devices * 8, rows), BF16),
            pltpu.VMEM((devices, meta_rows, BLOCK), BF16),
            pltpu.VMEM((LOW, build_table.shape[0] // LOW * width), BF16),
            pltpu.VMEM((devices, slot_rows, width), BF16),
            pltpu.VMEM((devices, slot_rows, width), BF16),
            pltpu.VMEM((groups, width), F32),
            pltpu.VMEM((groups, width), BF16),
            pltpu.VMEM((devices, GRP_DEV, width), BF16),
            pltpu.VMEM((8, BLOCK), F32),
            pltpu.VMEM((devices, 8, BLOCK), F32),
            pltpu.VMEM((inner // CORES,) + build_table.shape, BF16),
            pltpu.SemaphoreType.DMA((2, inner // CORES)),
            pltpu.SemaphoreType.DMA((inner // CORES,)),
        ]
        + [pltpu.SemaphoreType.DMA((devices,))] * 6,
        compiler_params=pltpu.CompilerParams(
            collective_id=0, has_side_effects=True, vmem_limit_bytes=56 * 1024 * 1024
        ),
    )(
        bounds,
        lengths,
        measures,
        pred_columns,
        destination.reshape(blocks, BLOCK),
        key_offset.reshape(blocks, BLOCK),
        group_ids.reshape(blocks, BLOCK),
        build_table,
    )
    return (sums, top[0, :TOPK])


def solution(mesh):
    both = ("section", "dom")
    inner = mesh.shape["dom"]
    devices = mesh.shape["section"] * inner
    return jax.shard_map(
        functools.partial(on_device, devices, inner),
        mesh=mesh,
        in_specs=(
            P(both, None),
            P(None, both),
            P(),
            P(both),
            P(both, None),
            P(both),
            P(both),
            P(both, None),
        ),
        out_specs=(P(both, None), P()),
        check_vma=False,
    )
```
